256 devices in a mesh: replica: 32 (over z, y_lo, core), fsdp: 8 (over y_hi, x).
Axes of the slice: x: 4, y: 4 (y_hi: 2, y_lo: 2; y = y_hi * 2 + y_lo), z: 8, core: 2. Of those that a mesh axis runs over, the one named last changes fastest.
Arguments:
- inputs: bfloat16 [32, 2048, 2560], P('replica', 'fsdp'), may hold values from -6 to 6
- targets: bfloat16 [32, 2048, 2560], P('replica', 'fsdp'), may hold values from -6 to 6
- masked: int32 [32, 2048], P('replica', 'fsdp'), may hold values 0 or 1
- step_index: int32 [], replicated, may hold values from 0 to 999
- weights: float32 [32, 2560, 2560], P('replica', 'fsdp'), may hold values from -0.125 to 0.125
- momentum: bfloat16 [32, 2560, 2560], P('replica', 'fsdp'), may hold values from -0.119628906 to 0.119628906
Outputs:
- new_weights: float32 [32, 2560, 2560], P('replica', 'fsdp')
- new_momentum: bfloat16 [32, 2560, 2560], P('replica', 'fsdp')
The draws below stay inside these ranges and needn't reach their ends.
All inputs are finite; a program needn't handle non-finite values. No bound on the sum of `masked` on one device may be relied on, other than what follows from the above.
Results may differ from the reference program's by a relative error of at most 0.015.
Values may be sent and summed in bfloat16 or wider, within the bound.
A program may use at most 128 MiB of HBM per device.

```python
import jax
import jax.numpy as jnp
from jax import lax

D_IN = 2560
D_OUT = 2560
SEQ = 2048
REPLICAS = 32
N_REPLICA = 32
N_FSDP = 8


def touch_ends(entries, own_key, least, high):
    extent = entries.shape
    spot = [jax.random.randint(jax.random.fold_in(own_key, axis), (), 0, extent[axis]) for axis in range(len(extent))]
    entries = entries.at[tuple(spot)].set(least)
    longest = extent.index(max(extent))
    spot[longest] = (spot[longest] + 1) % extent[longest]
    return entries.at[tuple(spot)].set(high)


def level_of(stream_key, shape, split, least, largest):
    def one(position, shards_of):
        heights = jax.random.uniform(jax.random.fold_in(jax.random.fold_in(stream_key, 6), position), (shards_of,), jnp.float32, least / len(split), largest / len(split))
        return jnp.repeat(jnp.exp(heights), shape[position] // shards_of).reshape((-1,) + (1,) * (len(shape) - position - 1))

    level = one(*split[0])
    for cut in split[1:]:
        level = level * one(*cut)
    return level


def centred(own_key, shape, deviation, bound, shards=(), dtype=jnp.bfloat16):
    level = level_of(own_key, shape, shards, -0.22, 0.18) if shards else 1.0
    array = jax.random.normal(own_key, shape, jnp.float32) * deviation * level
    return jnp.minimum(jnp.maximum(array, -bound), bound).astype(dtype)


def setup_inputs(seed: int = 0) -> dict:
    streams_of = jax.random.split(jax.random.key(seed), 7)
    inputs = centred(streams_of[0], (REPLICAS, SEQ, D_IN), 1.0, 6.0, ((0, 32), (1, 8)))
    targets = centred(streams_of[1], (REPLICAS, SEQ, D_OUT), 1.0, 6.0, ((0, 32), (1, 8)))
    masked = touch_ends((jax.random.randint(streams_of[2], (REPLICAS, SEQ), 0, 2) < 1).astype(jnp.int32), jax.random.fold_in(streams_of[2], 1), 0, 1)
    step_index = jax.random.randint(streams_of[3], (), 0, 1000).astype(jnp.int32)
    weights = centred(streams_of[4], (REPLICAS, D_IN, D_OUT), D_IN ** -0.5, 0.125, ((0, 32), (1, 8)), jnp.float32)
    momentum = centred(streams_of[5], (REPLICAS, D_IN, D_OUT), 0.02, 0.119628906, ((0, 32), (1, 8)))
    return dict(inputs=inputs, targets=targets, masked=masked, step_index=step_index, weights=weights, momentum=momentum)


def replica_grad(inputs_r, targets_r, masked_r, wbf_r):
    pred = jnp.dot(inputs_r, wbf_r, preferred_element_type=jnp.float32)
    seq_len = inputs_r.shape[0]
    scale = masked_r.astype(jnp.float32)[:, None] / seq_len
    resid = (scale * (pred - targets_r.astype(jnp.float32))).astype(jnp.bfloat16)
    x_blocks = inputs_r.reshape(N_FSDP, seq_len // N_FSDP, inputs_r.shape[1])
    r_blocks = resid.reshape(N_FSDP, seq_len // N_FSDP, resid.shape[1])

    def block_term(total, pair):
        x_block, r_block = pair
        term = lax.dot_general(x_block, r_block, (((0,), (0,)), ((), ())), preferred_element_type=jnp.float32)
        return (total + term.astype(jnp.bfloat16).astype(jnp.float32), None)
    start = jnp.zeros((inputs_r.shape[1], resid.shape[1]), jnp.float32)
    grad, unused = lax.scan(block_term, start, (x_blocks, r_blocks))
    return grad

def reference(inputs, targets, masked, step_index, weights, momentum):
    wbf = weights.astype(jnp.bfloat16)

    def per_replica(items):
        inputs_r, targets_r, masked_r, wbf_r, momentum_r = items
        grad = replica_grad(inputs_r, targets_r, masked_r, wbf_r)
        return (0.9 * momentum_r.astype(jnp.float32) + grad).astype(jnp.bfloat16)
    new_momentum = lax.map(per_replica, (inputs, targets, masked, wbf, momentum))
    levels = N_REPLICA.bit_length() - 1
    first = (2 ** (step_index % levels)).astype(jnp.int32)
    second = (2 ** ((step_index + 1) % levels)).astype(jnp.int32)
    half = (weights + jnp.roll(weights, first, axis=0)) / 2.0
    mixed = (half + jnp.roll(half, second, axis=0)) / 2.0
    rate = (step_index.astype(jnp.float32) + 1.0) / 500.0
    new_weights = mixed - rate * new_momentum.astype(jnp.float32)
    return (new_weights, new_momentum)
```

```python
import functools

import jax
import jax.numpy as jnp
from jax import lax
from jax.experimental import pallas as pl
from jax.experimental.pallas import tpu as pltpu
from jax.sharding import PartitionSpec as P

MESH = pl.DeviceIdType.MESH
BF = jnp.bfloat16
F32 = jnp.float32
COLS = 256
NT = 10
NJ = 5
ROWS = 320
SEQ = 256
HALF = 1280


def kernel(level, rate_ref, x_hbm, t_hbm, m_hbm, w_hbm, mom_hbm, neww_hbm, newm_hbm,
           win, wb, mom, xk, xt, tk, mk, wk, ps, pr, rb, gb, go, gr, hs, gh, ga, hb, gbuf,
           ld, xs, xr, xos, xor_, ts, tr, ms, mr, ws, wr, wss, wsr, pss, psr, rs, rr,
           gs, grr, hss, hsr, as_, ar, bs, br, outs):
    r = lax.axis_index("replica")
    f = lax.axis_index("fsdp")
    c = lax.rem(r, 2)
    pair = r - c
    yh = f // 4
    x = lax.rem(f, 4)
    lo = lax.rem(x, 2)
    hi = x // 2
    xo = x + 1 - 2 * lo
    xs_ = 3 - x
    o = lax.rem(lo + hi, 2)
    home = c == yh

    def dev(core, y, xx):
        return (pair + core, y * 4 + xx)

    def other(offset):
        return (lax.rem(r + offset, 32), f)

    def remote(src, dst, ss, rsem, to):
        return pltpu.make_async_remote_copy(src_ref=src, dst_ref=dst, send_sem=ss, recv_sem=rsem,
                                            device_id=to, device_id_type=MESH)

    def arrived(dst, rsem):
        remote(dst, dst, rsem, rsem, dev(1 - c, yh, x)).wait_recv()

    w_loads = [pltpu.make_async_copy(w_hbm.at[:, pl.ds(t * COLS, COLS)], win.at[t], ld.at[t]) for t in range(NT)]
    for copy in w_loads:
        copy.start()
    m_load = pltpu.make_async_copy(mom_hbm, mom, ld.at[NT])
    m_load.start()

    near, later = 2**level, 2 ** ((level + 1) % 5)
    if level == 3:
        offsets = [8, 16, 24]
    else:
        offsets = sorted({near, 32 - near, later, 32 - later})
    barrier = pltpu.get_barrier_semaphore()
    peers = [dev(1 - c, yh, x), dev(c, 1 - yh, x), dev(1 - c, 1 - yh, x), dev(c, yh, xs_)]
    peers += [dev(a, b, xo) for a in (0, 1) for b in (0, 1)]
    peers += [other(a) for a in offsets]
    for peer in peers:
        pl.semaphore_signal(barrier, inc=1, device_id=peer, device_id_type=MESH)
    pl.semaphore_wait(barrier, len(peers))

    x_to = xk.at[yh * 2 + lo]
    x_away = []
    for k in range(2):
        src = x_hbm.at[:, pl.ds(k * HALF, HALF)]
        mine = jnp.logical_and(home, c == k)
        x_away.append((jnp.logical_not(mine), remote(src, x_to, xs.at[k], xr.at[yh], dev(k, c, x))))

        @pl.when(mine)
        def _(src=src):
            pltpu.make_async_copy(src, x_to, xr.at[yh]).start()

        @pl.when(jnp.logical_not(mine))
        def _(copy=x_away[-1][1]):
            copy.start()

    def send_w(j):
        keep = wb.at[o * NJ + j]
        give = wb.at[(1 - o) * NJ + j]
        dst = wk.at[j, pl.ds(pl.multiple_of(x * ROWS, ROWS), ROWS)]
        first = remote(keep, dst, ws.at[0, j], wr.at[lo, j], dev(yh, c, x))
        second = remote(give, dst, ws.at[1, j], wr.at[lo, j], dev(yh, c, xo))
        return keep, dst, first, second

    for t in range(NT):
        w_loads[t].wait()
        wb[t] = win[t].astype(BF)

    for j in range(NJ):
        keep, dst, first, second = send_w(j)

        @pl.when(home)
        def _(keep=keep, dst=dst, j=j):
            pltpu.make_async_copy(keep, dst, wr.at[lo, j]).start()

        @pl.when(jnp.logical_not(home))
        def _(first=first):
            first.start()

        second.start()

    if level == 3:
        member = r // 8
        quarter = ROWS // 4

        def part(q):
            return pl.ds(pl.multiple_of(q * quarter, 16), quarter)

        a_copies = []
        for d in range(1, 4):
            q = lax.rem(member + d, 4)
            a_copies.append(remote(wb.at[:, part(q)], ga.at[:, pl.ds((d - 1) * quarter, quarter)],
                                   as_.at[d - 1], ar.at[d - 1], other(8 * d)))
    else:
        a_copies = [remote(wb.at[t], ga.at[t], as_.at[t], ar.at[t], other(near)) for t in range(NT)]
    for copy in a_copies:
        copy.start()

    t_cols = [pl.ds(pl.multiple_of(h * HALF, HALF), HALF) for h in (o, 1 - o)]
    t_dst = tk.at[pl.ds(pl.multiple_of(lo * SEQ, SEQ), SEQ)]
    m_dst = mk.at[pl.ds(pl.multiple_of(lo * SEQ, SEQ), SEQ)]
    t_first = remote(t_hbm.at[:, t_cols[0]], t_dst, ts.at[0], tr.at[lo], dev(yh, c, x))
    t_second = remote(t_hbm.at[:, t_cols[1]], t_dst, ts.at[1], tr.at[lo], dev(yh, c, xo))
    m_first = remote(m_hbm, m_dst, ms.at[0], mr.at[lo], dev(yh, c, x))
    m_second = remote(m_hbm, m_dst, ms.at[1], mr.at[lo], dev(yh, c, xo))

    @pl.when(home)
    def _():
        pltpu.make_async_copy(t_hbm.at[:, t_cols[0]], t_dst, tr.at[lo]).start()
        pltpu.make_async_copy(m_hbm, m_dst, mr.at[lo]).start()

    @pl.when(jnp.logical_not(home))
    def _():
        t_first.start()
        m_first.start()

    t_second.start()
    m_second.start()

    def turn(slot):
        xt[slot] = xk[slot].T

    relays = []
    for step in range(2):
        ry = yh if step == 0 else 1 - yh
        slot = ry * 2 + lo
        arrived(xk.at[slot], xr.at[ry])
        copy = remote(xk.at[slot], xk.at[slot], xos.at[step], xor_.at[ry], dev(c, yh, xo))
        copy.start()
        relays.append(copy)
        turn(slot)

    mine_rows = pl.ds(pl.multiple_of(hi * 2 * ROWS, 2 * ROWS), 2 * ROWS)
    their_rows = pl.ds(pl.multiple_of((1 - hi) * 2 * ROWS, 2 * ROWS), 2 * ROWS)
    w_on = []
    for j in range(NJ):
        for side in range(2):
            arrived(wk.at[j, pl.ds(pl.multiple_of(hi * 2 * ROWS, 2 * ROWS) + side * ROWS, ROWS)], wr.at[side, j])
        copy = remote(wk.at[j, mine_rows], wk.at[j, mine_rows], wss.at[j], wsr.at[j], dev(c, yh, xs_))
        copy.start()
        w_on.append(copy)

    for step in range(2):
        ry = yh if step == 0 else 1 - yh
        slot = ry * 2 + (1 - lo)
        arrived(xk.at[slot], xor_.at[ry])
        turn(slot)

    core = dev(1 - c, yh, x)
    half_rows = [pl.ds(pl.multiple_of(h * 512, 512), 512) for h in (c, 1 - c)]
    p_copies, r_copies, g_copies, h_copies = [], [], [], []

    def step_p(j):
        arrived(wk.at[j, their_rows], wsr.at[j])

        def one(ry):
            @pl.loop(0, 2)
            def _(side):
                b = ry * 2 + side
                rows = pl.ds(pl.multiple_of(b * SEQ, SEQ), SEQ)
                ps[j, rows] = jnp.dot(xk[b], wk[j], preferred_element_type=F32)

        one(1 - c)
        copy = remote(ps.at[j, half_rows[1]], pr.at[j], pss.at[j], psr.at[j], core)
        copy.start()
        p_copies.append(copy)
        one(c)

    def step_r(j):
        if j == 0:
            for side in range(2):
                arrived(tk.at[pl.ds(side * SEQ, SEQ)], tr.at[side])
                arrived(mk.at[pl.ds(side * SEQ, SEQ)], mr.at[side])
        arrived(pr.at[j], psr.at[j])

        @pl.loop(0, 8)
        def _(i):
            rows = pl.ds(pl.multiple_of(i * 64, 64), 64)
            full = pl.ds(pl.multiple_of(c * 512 + i * 64, 64), 64)
            scale = mk[rows].astype(F32)
            scale = jnp.concatenate([scale, scale], axis=1)
            pred = ps[j, full] + pr[j, rows]
            goal = tk[rows, pl.ds(j * COLS, COLS)].astype(F32)
            rb[j, full] = (scale * (pred - goal)).astype(BF)

        copy = remote(rb.at[j, half_rows[0]], rb.at[j, half_rows[0]], rs.at[j], rr.at[j], core)
        copy.start()
        r_copies.append(copy)

    def product(j, row):
        total = None
        for b in range(4):
            term = jnp.dot(xt[b, pl.ds(pl.multiple_of(row, ROWS), ROWS)], rb[j, pl.ds(b * SEQ, SEQ)],
                           preferred_element_type=F32)
            total = term if total is None else total + term
        return total

    def step_g(j):
        arrived(rb.at[j, half_rows[1]], rr.at[j])

        @pl.loop(0, 2)
        def _(i):
            gb[j, pl.ds(pl.multiple_of(i * ROWS, ROWS), ROWS)] = product(j, ((1 - hi) * 2 + i) * ROWS).astype(BF)

        copy = remote(gb.at[j], gr.at[j], gs.at[j], grr.at[j], dev(c, yh, xs_))
        copy.start()
        g_copies.append(copy)

        @pl.loop(0, 2)
        def _(i):
            go[j, pl.ds(pl.multiple_of(i * ROWS, ROWS), ROWS)] = product(j, (hi * 2 + i) * ROWS)

    def step_h(j):
        arrived(gr.at[j], grr.at[j])

        def one(side):
            @pl.loop(0, 5)
            def _(i):
                rows = pl.ds(pl.multiple_of(side * ROWS + i * 64, 64), 64)
                hs[j, rows] = (go[j, rows] + gr[j, rows].astype(F32)).astype(BF)
            return hs.at[j, pl.ds(pl.multiple_of(side * ROWS, ROWS), ROWS)]

        dst = gh.at[o * NJ + j]
        sem = hsr.at[o * NJ + j]
        copy = remote(one(1 - lo), dst, hss.at[1, j], sem, dev(yh, c, xo))
        copy.start()
        own = one(lo)
        first = remote(own, dst, hss.at[0, j], sem, dev(yh, c, x))
        h_copies.append((first, copy))

        @pl.when(home)
        def _():
            pltpu.make_async_copy(own, dst, sem).start()

        @pl.when(jnp.logical_not(home))
        def _():
            first.start()

    b_copies = []

    def gossip_half(t):
        arrived(ga.at[t], ar.at[t])

        @pl.loop(0, 5)
        def _(i):
            rows = pl.ds(pl.multiple_of(i * 64, 64), 64)
            half = (win[t, rows] + ga[t, rows].astype(F32)) * 0.5
            win[t, rows] = half
            hb[t, rows] = half.astype(BF)

        copy = remote(hb.at[t], gbuf.at[t], bs.at[t], br.at[t], other(later))
        copy.start()
        b_copies.append(copy)

    def gossip_quarter():
        for d in range(3):
            arrived(ga.at[:, pl.ds(d * quarter, quarter)], ar.at[d])

        @pl.loop(0, NT)
        def _(t):
            total = win[t, part(member)]
            for d in range(3):
                total += ga[t, pl.ds(d * quarter, quarter)].astype(F32)
            hb[t, part(member)] = (total * 0.25).astype(BF)

        for d in range(1, 4):
            copy = remote(hb.at[:, part(member)], hb.at[:, part(member)], bs.at[d - 1], br.at[d - 1], other(8 * d))
            copy.start()
            b_copies.append(copy)

    for j in range(NJ + 3):
        if j < NJ:
            step_p(j)
        if 1 <= j < NJ + 1:
            step_r(j - 1)
        if 2 <= j < NJ + 2:
            step_g(j - 2)
        if 3 <= j:
            step_h(j - 3)
        if level == 3:
            if j == NJ:
                gossip_quarter()
        elif 1 <= j <= 5:
            gossip_half(2 * j - 2)
            gossip_half(2 * j - 1)

    m_load.wait()
    rate = rate_ref[0]
    if level == 3:
        for d in range(1, 4):
            arrived(hb.at[:, part(lax.rem(member + 4 - d, 4))], br.at[d - 1])
    out_copies = []
    for j in range(NJ):
        for t in (j, NJ + j):
            if level != 3:
                arrived(gbuf.at[t], br.at[t])
            arrived(gh.at[t], hsr.at[t])

            @pl.loop(0, 5)
            def _(i, t=t):
                rows = pl.ds(pl.multiple_of(i * 64, 64), 64)
                cols = pl.ds(t * COLS, COLS)
                moved = (0.9 * mom[rows, cols].astype(F32) + gh[t, rows].astype(F32)).astype(BF)
                mom[rows, cols] = moved
                if level == 3:
                    mixed = hb[t, rows].astype(F32)
                else:
                    mixed = (win[t, rows] + gbuf[t, rows].astype(F32)) * 0.5
                win[t, rows] = mixed - rate * moved.astype(F32)

            cols = pl.ds(t * COLS, COLS)
            for copy in (pltpu.make_async_copy(win.at[t], neww_hbm.at[:, cols], outs.at[0, t]),
                         pltpu.make_async_copy(mom.at[:, cols], newm_hbm.at[:, cols], outs.at[1, t])):
                copy.start()
                out_copies.append(copy)

    for away, copy in x_away:
        pl.when(away)(copy.wait_send)
    for j in range(NJ):
        keep, dst, first, second = send_w(j)
        pl.when(jnp.logical_not(home))(first.wait_send)
        second.wait_send()
        first, second = h_copies[j]
        pl.when(jnp.logical_not(home))(first.wait_send)
        second.wait_send()

    @pl.when(jnp.logical_not(home))
    def _():
        t_first.wait_send()
        m_first.wait_send()

    for copy in [t_second, m_second, *relays, *w_on, *p_copies, *r_copies, *g_copies, *a_copies, *b_copies]:
        copy.wait_send()
    for copy in out_copies:
        copy.wait()


def update(level, rate, tokens, goals, marks, shard, momentum):
    dma = pltpu.SemaphoreType.DMA
    anywhere = pl.BlockSpec(memory_space=pl.ANY)
    vm = pltpu.VMEM
    return pl.pallas_call(
        functools.partial(kernel, level),
        out_shape=(
            jax.ShapeDtypeStruct((ROWS, NT * COLS), F32),
            jax.ShapeDtypeStruct((ROWS, NT * COLS), BF),
        ),
        in_specs=[pl.BlockSpec(memory_space=pltpu.SMEM)] + [anywhere] * 5,
        out_specs=(anywhere, anywhere),
        scratch_shapes=[
            vm((NT, ROWS, COLS), F32),
            vm((NT, ROWS, COLS), BF),
            vm((ROWS, NT * COLS), BF),
            vm((4, SEQ, HALF), BF),
            vm((4, HALF, SEQ), BF),
            vm((2 * SEQ, HALF), BF),
            vm((2 * SEQ, 128), BF),
            vm((NJ, HALF, COLS), BF),
            vm((NJ, 4 * SEQ, COLS), F32),
            vm((NJ, 2 * SEQ, COLS), F32),
            vm((NJ, 4 * SEQ, COLS), BF),
            vm((NJ, 2 * ROWS, COLS), BF),
            vm((NJ, 2 * ROWS, COLS), F32),
            vm((NJ, 2 * ROWS, COLS), BF),
            vm((NJ, 2 * ROWS, COLS), BF),
            vm((NT, ROWS, COLS), BF),
            vm((NT, ROWS, COLS), BF),
            vm((NT, ROWS, COLS), BF),
            vm((NT, ROWS, COLS), BF),
            dma((NT + 1,)),
            dma((2,)), dma((2,)),
            dma((2,)), dma((2,)),
            dma((2,)), dma((2,)),
            dma((2,)), dma((2,)),
            dma((2, NJ)), dma((2, NJ)),
            dma((NJ,)), dma((NJ,)),
            dma((NJ,)), dma((NJ,)),
            dma((NJ,)), dma((NJ,)),
            dma((NJ,)), dma((NJ,)),
            dma((2, NJ)), dma((NT,)),
            dma((NT,)), dma((NT,)),
            dma((NT,)), dma((NT,)),
            dma((2, NT)),
        ],
        compiler_params=pltpu.CompilerParams(
            collective_id=level, has_side_effects=True, vmem_limit_bytes=60 * 2**20
        ),
        name=f"update_{level}",
    )(rate, tokens, goals, marks, shard, momentum)


def local(inputs, targets, masked, step_index, weights, momentum):
    marks = jnp.broadcast_to((masked[0].astype(F32) / 2048.0).astype(BF)[:, None], (SEQ, 128))
    rate = ((step_index.astype(F32) + 1.0) / 500.0).reshape(1)
    branches = [functools.partial(update, level) for level in range(5)]
    new_weights, new_momentum = lax.switch(
        step_index % 5, branches, rate, inputs[0], targets[0], marks, weights[0], momentum[0]
    )
    return new_weights[None], new_momentum[None]


def solution(mesh):
    in_specs = (
        P("replica", "fsdp", None),
        P("replica", "fsdp", None),
        P("replica", "fsdp"),
        P(),
        P("replica", "fsdp", None),
        P("replica", "fsdp", None),
    )
    out_specs = (P("replica", "fsdp", None), P("replica", "fsdp", None))
    return jax.shard_map(local, mesh=mesh, in_specs=in_specs, out_specs=out_specs, check_vma=False)
```

```python
import functools

import jax
import jax.numpy as jnp
from jax import lax
from jax.experimental import pallas as pl
from jax.experimental.pallas import tpu as pltpu
from jax.sharding import PartitionSpec as P

MESH = pl.DeviceIdType.MESH
BF = jnp.bfloat16
F32 = jnp.float32
COLS = 256
NT = 10
NJ = 5
ROWS = 320
SEQ = 256
HALF = 1280


def span(start, size):
    return pl.ds(pl.multiple_of(start, size), size)


def kernel(level, rate_ref, x_hbm, t_hbm, m_hbm, w_hbm, mom_hbm, neww_hbm, newm_hbm,
           win, wb, mom, xk, xt, tk, mk, wk, ps, pr, rb, gb, go, gr, hs, gh, ga, hb, gbuf,
           ld, xs, xr, xos, xor_, ts, tr, ms, mr, ws, wr, wss, wsr, pss, psr, rs, rr,
           gs, grr, hss, hsr, as_, ar, bs, br, outs):
    r = lax.axis_index("replica")
    f = lax.axis_index("fsdp")
    c = lax.rem(r, 2)
    pair = r - c
    yh = f // 4
    x = lax.rem(f, 4)
    lo = lax.rem(x, 2)
    hi = x // 2
    xo = x + 1 - 2 * lo
    across = 3 - x
    o = lax.rem(lo + hi, 2)
    home = c == yh
    away = jnp.logical_not(home)

    def dev(core, y, xx):
        return (pair + core, y * 4 + xx)

    def other(offset):
        return (lax.rem(r + offset, 32), f)

    partner = dev(1 - c, yh, x)
    worker = dev(yh, c, x)
    worker_o = dev(yh, c, xo)
    side_o = dev(c, yh, xo)
    side_s = dev(c, yh, across)

    def remote(src, dst, ss, rsem, to):
        return pltpu.make_async_remote_copy(src_ref=src, dst_ref=dst, send_sem=ss, recv_sem=rsem,
                                            device_id=to, device_id_type=MESH)

    def arrived(dst, rsem, site=None):
        remote(dst, dst, rsem, rsem, partner).wait_recv()

    def local_or_remote(src, dst, ss, rsem):
        @pl.when(home)
        def _():
            pltpu.make_async_copy(src, dst, rsem).start()

        @pl.when(away)
        def _():
            remote(src, dst, ss, rsem, worker).start()

    def w_load(t):
        return pltpu.make_async_copy(w_hbm.at[:, span(t * COLS, COLS)], win.at[t], ld.at[t])

    @pl.loop(0, NJ)
    def _(j):
        w_load(o * NJ + j).start()

    @pl.loop(0, NJ)
    def _(j):
        w_load((1 - o) * NJ + j).start()

    m_load = pltpu.make_async_copy(mom_hbm, mom, ld.at[NT])
    m_load.start()

    near, later = 2**level, 2 ** ((level + 1) % 5)
    if level == 3:
        offsets = [8, 16, 24]
    else:
        offsets = sorted({near, 32 - near, later, 32 - later})
    barrier = pltpu.get_barrier_semaphore()
    peers = [partner, dev(c, 1 - yh, x), dev(1 - c, 1 - yh, x), side_s]
    peers += [dev(a, b, xo) for a in (0, 1) for b in (0, 1)]
    peers += [other(a) for a in offsets]
    for peer in peers:
        pl.semaphore_signal(barrier, inc=1, device_id=peer, device_id_type=MESH)
    pl.semaphore_wait(barrier, len(peers))

    def x_send(k):
        return remote(x_hbm.at[:, span(k * HALF, HALF)], xk.at[yh * 2 + lo], xs.at[k], xr.at[yh], dev(k, c, x))

    @pl.loop(0, 2)
    def _(k):
        mine = jnp.logical_and(home, c == k)

        @pl.when(mine)
        def _():
            pltpu.make_async_copy(x_hbm.at[:, span(k * HALF, HALF)], xk.at[yh * 2 + lo], xr.at[yh]).start()

        @pl.when(jnp.logical_not(mine))
        def _():
            x_send(k).start()

    def own_rows(j):
        return wk.at[j, span(x * ROWS, ROWS)]

    def o_rows(j):
        return wk.at[j, span(xo * ROWS, ROWS)]

    def w_keep(j):
        return remote(wb.at[o * NJ + j], own_rows(j), ws.at[0, j], wr.at[lo, j], worker)

    def w_give(j):
        return remote(wb.at[(1 - o) * NJ + j], own_rows(j), ws.at[1, j], wr.at[lo, j], worker_o)

    def w_own_on(src, j):
        return remote(src, own_rows(j), wss.at[0, j], wsr.at[lo, j], side_s)

    def w_o_on(j):
        return remote(o_rows(j), o_rows(j), wss.at[1, j], wsr.at[1 - lo, j], side_s)

    def cast(t):
        w_load(t).wait()
        wb[t] = win[t].astype(BF)

    def t_cols(side, j):
        half = o if side == 0 else 1 - o
        return t_hbm.at[:, span(half * HALF + j * COLS, COLS)]

    t_dst = span(lo * SEQ, SEQ)

    def t_keep(j):
        return remote(t_cols(0, j), tk.at[j, t_dst], ts.at[0, j], tr.at[lo, j], worker)

    def t_give(j):
        return remote(t_cols(1, j), tk.at[j, t_dst], ts.at[1, j], tr.at[lo, j], worker_o)

    m_dst = mk.at[span(lo * SEQ, SEQ)]
    m_keep = remote(m_hbm, m_dst, ms.at[0], mr.at[lo], worker)
    m_give = remote(m_hbm, m_dst, ms.at[1], mr.at[lo], worker_o)

    @pl.loop(0, NJ)
    def _(j):
        t = o * NJ + j
        cast(t)

        @pl.when(home)
        def _():
            pltpu.make_async_copy(wb.at[t], own_rows(j), wr.at[lo, j]).start()
            w_own_on(wb.at[t], j).start()
            pltpu.make_async_copy(t_cols(0, j), tk.at[j, t_dst], tr.at[lo, j]).start()

        @pl.when(away)
        def _():
            w_keep(j).start()

    def turn(slot):
        xt[:, span(slot * SEQ, SEQ)] = xk[slot].T

    def x_on(ry):
        slot = ry * 2 + lo
        return remote(xk.at[slot], xk.at[slot], xos.at[ry], xor_.at[ry], side_o)

    arrived(xk.at[yh * 2 + lo], xr.at[yh], 0)
    x_on(yh).start()

    def give(j):
        w_give(j).start()
        t_give(j).start()

        @pl.when(away)
        def _():
            t_keep(j).start()

    cast((1 - o) * NJ)

    @pl.when(home)
    def _():
        give(0)
        m_give.start()
        pltpu.make_async_copy(m_hbm, m_dst, mr.at[lo]).start()

    @pl.loop(1, NJ)
    def _(j):
        cast((1 - o) * NJ + j)

    if level == 3:
        member = r // 8
        quarter = ROWS // 4

        def part(q):
            return span(q * quarter, quarter)

        def a_copy(d):
            q = lax.rem(member + d, 4)
            return remote(wb.at[:, part(q)], ga.at[:, part(d - 1)], as_.at[d - 1], ar.at[d - 1], other(8 * d))

        def b_copy(d):
            return remote(hb.at[:, part(member)], hb.at[:, part(member)], bs.at[d - 1], br.at[d - 1], other(8 * d))

        first_copies, second_copies = (1, 4), (1, 4)
    else:

        def a_copy(t):
            return remote(wb.at[t], ga.at[t], as_.at[t], ar.at[t], other(near))

        def b_copy(t):
            return remote(hb.at[t], gbuf.at[t], bs.at[t], br.at[t], other(later))

        first_copies, second_copies = (0, NT), (0, NT)

    def first_transfer():
        @pl.loop(*first_copies)
        def _(t):
            a_copy(t).start()

    if level >= 2:
        first_transfer()
    turn(yh * 2 + lo)
    arrived(xk.at[(1 - yh) * 2 + lo], xr.at[1 - yh], 1)
    x_on(1 - yh).start()

    @pl.when(home)
    def _():
        pl.loop(1, NJ)(give)

    @pl.when(away)
    def _():
        give(0)
        m_keep.start()
        m_give.start()

    turn((1 - yh) * 2 + lo)

    def gossip_half(t):
        arrived(ga.at[t], ar.at[t], 40 + t)

        @pl.loop(0, 5)
        def _(i):
            rows = span(i * 64, 64)
            half = (win[t, rows] + ga[t, rows].astype(F32)) * 0.5
            win[t, rows] = half
            hb[t, rows] = half.astype(BF)

        b_copy(t).start()

    def gossip_quarter():
        for d in range(3):
            arrived(ga.at[:, part(d)], ar.at[d], 40 + d)

        @pl.loop(0, NT)
        def _(t):
            total = win[t, part(member)]
            for d in range(3):
                total += ga[t, part(d)].astype(F32)
            hb[t, part(member)] = (total * 0.25).astype(BF)

        @pl.loop(*second_copies)
        def _(d):
            b_copy(d).start()

    def forward(j):
        arrived(o_rows(j), wr.at[1 - lo, j], 50 + j)
        w_o_on(j).start()

    @pl.when(away)
    def _():
        @pl.loop(0, NJ)
        def _(j):
            arrived(own_rows(j), wr.at[lo, j], 2)
            w_own_on(own_rows(j), j).start()

        pl.loop(1, NJ)(give)

    arrived(xk.at[yh * 2 + 1 - lo], xor_.at[yh], 3)
    turn(yh * 2 + 1 - lo)
    if level == 2:

        @pl.loop(0, 4)
        def _(t):
            gossip_half(t)

    forward(0)
    arrived(xk.at[(1 - yh) * 2 + 1 - lo], xor_.at[1 - yh], 4)

    def p_copy(j):
        return remote(ps.at[j, span((1 - c) * 512, 512)], pr.at[j], pss.at[j], psr.at[j], partner)

    def step_p(j):
        @pl.when(home)
        def _():
            arrived(own_rows(j), wr.at[lo, j], 5)

        arrived(wk.at[j, span(across * ROWS, ROWS)], wsr.at[1 - lo, j], 60 + j)
        arrived(wk.at[j, span((3 - xo) * ROWS, ROWS)], wsr.at[lo, j], 70 + j)

        @pl.loop(0, 4)
        def _(i):
            b = lax.rem((1 - c) * 2 + i, 4)
            ps[j, span(b * SEQ, SEQ)] = jnp.dot(xk[b], wk[j], preferred_element_type=F32)

            @pl.when(i == 1)
            def _():
                p_copy(j).start()

    def r_copy(j):
        ref = rb.at[j, span(c * 512, 512)]
        return remote(ref, ref, rs.at[j], rr.at[j], partner)

    def step_r(j):
        @pl.when(j == 0)
        def _():
            for side in range(2):
                arrived(mk.at[pl.ds(side * SEQ, SEQ)], mr.at[side], 6)

        arrived(tk.at[j, span(lo * SEQ, SEQ)], tr.at[lo, j], 80 + j)
        arrived(tk.at[j, span((1 - lo) * SEQ, SEQ)], tr.at[1 - lo, j], 80 + j)
        arrived(pr.at[j], psr.at[j], 90 + j)

        @pl.loop(0, 8)
        def _(i):
            rows = span(i * 64, 64)
            full = span(c * 512 + i * 64, 64)
            scale = mk[rows].astype(F32)
            scale = jnp.concatenate([scale, scale], axis=1)
            pred = ps[j, full] + pr[j, rows]
            rb[j, full] = (scale * (pred - tk[j, rows].astype(F32))).astype(BF)

        r_copy(j).start()

    def g_copy(j):
        return remote(gb.at[j], gr.at[j], gs.at[j], grr.at[j], side_s)

    def step_g(j):
        arrived(rb.at[j, span((1 - c) * 512, 512)], rr.at[j], 100 + j)

        @pl.loop(0, 4)
        def _(i):
            half = jnp.where(i < 2, 1 - hi, hi)
            row = half * 2 * ROWS + lax.rem(i, 2) * ROWS
            value = jnp.dot(xt[span(row, ROWS)], rb[j], preferred_element_type=F32)
            rows = span(lax.rem(i, 2) * ROWS, ROWS)

            @pl.when(i < 2)
            def _():
                gb[j, rows] = value.astype(BF)

            @pl.when(i >= 2)
            def _():
                go[j, rows] = value

            @pl.when(i == 1)
            def _():
                g_copy(j).start()

    def h_give(j):
        return remote(hs.at[j, span((1 - lo) * ROWS, ROWS)], gh.at[o * NJ + j], hss.at[1, j], hsr.at[o * NJ + j], worker_o)

    def h_keep(j):
        return remote(hs.at[j, span(lo * ROWS, ROWS)], gh.at[o * NJ + j], hss.at[0, j], hsr.at[o * NJ + j], worker)

    def step_h(j):
        arrived(gr.at[j], grr.at[j], 110 + j)

        @pl.loop(0, 10)
        def _(i):
            rows = span(i * 64, 64)
            hs[j, rows] = (go[j, rows] + gr[j, rows].astype(F32)).astype(BF)

        h_give(j).start()
        local_or_remote(hs.at[j, span(lo * ROWS, ROWS)], gh.at[o * NJ + j], hss.at[0, j], hsr.at[o * NJ + j])

    rate = rate_ref[0]

    def out_w(t):
        return pltpu.make_async_copy(win.at[t], neww_hbm.at[:, span(t * COLS, COLS)], outs.at[0, t])

    def out_m(t):
        cols = span(t * COLS, COLS)
        return pltpu.make_async_copy(mom.at[:, cols], newm_hbm.at[:, cols], outs.at[1, t])

    def finish(t):
        arrived(gh.at[t], hsr.at[t], 120 + t)
        if level != 3:
            arrived(gbuf.at[t], br.at[t], 130 + t)

        @pl.loop(0, 5)
        def _(i):
            rows = span(i * 64, 64)
            cols = span(t * COLS, COLS)
            moved = (0.9 * mom[rows, cols].astype(F32) + gh[t, rows].astype(F32)).astype(BF)
            mom[rows, cols] = moved
            if level == 3:
                mixed = hb[t, rows].astype(F32)
            else:
                mixed = (win[t, rows] + gbuf[t, rows].astype(F32)) * 0.5
            win[t, rows] = mixed - rate * moved.astype(F32)

        out_w(t).start()
        out_m(t).start()

    @pl.loop(0, NJ + 4)
    def _(i):
        @pl.when(i < NJ)
        def _():
            step_p(i)

            @pl.when(i == 0)
            def _():
                turn((1 - yh) * 2 + 1 - lo)
                if level < 2:
                    first_transfer()

            @pl.when(i < NJ - 1)
            def _():
                forward(i + 1)

            step_r(i)
            step_g(i)

        @pl.when(jnp.logical_and(i >= 2, i < NJ + 2))
        def _():
            step_h(i - 2)

        if level == 3:

            @pl.when(i == 1)
            def _():
                gossip_quarter()
        elif level == 2:

            @pl.when(i < 2)
            def _():
                @pl.loop(4 + 3 * i, 7 + 3 * i)
                def _(t):
                    gossip_half(t)
        else:
            lag = 1 if level < 2 else 0

            @pl.when(jnp.logical_and(i >= lag, i < lag + 5))
            def _():
                @pl.loop(2 * (i - lag), 2 * (i - lag) + 2)
                def _(t):
                    gossip_half(t)

        @pl.when(i == 4)
        def _():
            m_load.wait()
            if level == 3:
                for d in range(1, 4):
                    arrived(hb.at[:, part(lax.rem(member + 4 - d, 4))], br.at[d - 1], 130)

        @pl.when(i >= 4)
        def _():
            @pl.loop(0, 2)
            def _(h):
                finish(h * NJ + i - 4)

    @pl.loop(0, 2)
    def _(k):
        @pl.when(jnp.logical_not(jnp.logical_and(home, c == k)))
        def _():
            x_send(k).wait_send()

        x_on(k).wait_send()

    m_give.wait_send()
    pl.when(away)(m_keep.wait_send)

    @pl.loop(0, NJ)
    def _(j):
        @pl.when(away)
        def _():
            w_keep(j).wait_send()
            t_keep(j).wait_send()
            h_keep(j).wait_send()

        for copy in (w_give(j), t_give(j), h_give(j), w_own_on(own_rows(j), j), w_o_on(j), p_copy(j), r_copy(j), g_copy(j)):
            copy.wait_send()

    @pl.loop(*first_copies)
    def _(t):
        a_copy(t).wait_send()

    @pl.loop(*second_copies)
    def _(t):
        b_copy(t).wait_send()

    @pl.loop(0, NT)
    def _(t):
        out_w(t).wait()
        out_m(t).wait()


def update(level, rate, tokens, goals, marks, shard, momentum):
    dma = pltpu.SemaphoreType.DMA
    anywhere = pl.BlockSpec(memory_space=pl.ANY)
    vm = pltpu.VMEM
    return pl.pallas_call(
        functools.partial(kernel, level),
        out_shape=(
            jax.ShapeDtypeStruct((ROWS, NT * COLS), F32),
            jax.ShapeDtypeStruct((ROWS, NT * COLS), BF),
        ),
        in_specs=[pl.BlockSpec(memory_space=pltpu.SMEM)] + [anywhere] * 5,
        out_specs=(anywhere, anywhere),
        scratch_shapes=[
            vm((NT, ROWS, COLS), F32),
            vm((NT, ROWS, COLS), BF),
            vm((ROWS, NT * COLS), BF),
            vm((4, SEQ, HALF), BF),
            vm((HALF, 4 * SEQ), BF),
            vm((NJ, 2 * SEQ, COLS), BF),
            vm((2 * SEQ, 128), BF),
            vm((NJ, HALF, COLS), BF),
            vm((NJ, 4 * SEQ, COLS), F32),
            vm((NJ, 2 * SEQ, COLS), F32),
            vm((NJ, 4 * SEQ, COLS), BF),
            vm((NJ, 2 * ROWS, COLS), BF),
            vm((NJ, 2 * ROWS, COLS), F32),
            vm((NJ, 2 * ROWS, COLS), BF),
            vm((NJ, 2 * ROWS, COLS), BF),
            vm((NT, ROWS, COLS), BF),
            vm((NT, ROWS, COLS), BF),
            vm((NT, ROWS, COLS), BF),
            vm((NT, ROWS, COLS), BF),
            dma((NT + 1,)),
            dma((2,)), dma((2,)),
            dma((2,)), dma((2,)),
            dma((2, NJ)), dma((2, NJ)),
            dma((2,)), dma((2,)),
            dma((2, NJ)), dma((2, NJ)),
            dma((2, NJ)), dma((2, NJ)),
            dma((NJ,)), dma((NJ,)),
            dma((NJ,)), dma((NJ,)),
            dma((NJ,)), dma((NJ,)),
            dma((2, NJ)), dma((NT,)),
            dma((NT,)), dma((NT,)),
            dma((NT,)), dma((NT,)),
            dma((2, NT)),
        ],
        compiler_params=pltpu.CompilerParams(
            collective_id=level, has_side_effects=True, vmem_limit_bytes=60 * 2**20
        ),
        name=f"update_{level}",
    )(rate, tokens, goals, marks, shard, momentum)


def local(inputs, targets, masked, step_index, weights, momentum):
    marks = jnp.broadcast_to((masked[0].astype(F32) / 2048.0).astype(BF)[:, None], (SEQ, 128))
    rate = ((step_index.astype(F32) + 1.0) / 500.0).reshape(1)
    branches = [functools.partial(update, level) for level in range(5)]
    new_weights, new_momentum = lax.switch(
        step_index % 5, branches, rate, inputs[0], targets[0], marks, weights[0], momentum[0]
    )
    return new_weights[None], new_momentum[None]


def solution(mesh):
    in_specs = (
        P("replica", "fsdp", None),
        P("replica", "fsdp", None),
        P("replica", "fsdp"),
        P(),
        P("replica", "fsdp", None),
        P("replica", "fsdp", None),
    )
    out_specs = (P("replica", "fsdp", None), P("replica", "fsdp", None))
    return jax.shard_map(local, mesh=mesh, in_specs=in_specs, out_specs=out_specs, check_vma=False)
```

```python
import functools

import jax
import jax.numpy as jnp
from jax import lax
from jax.experimental import pallas as pl
from jax.experimental.pallas import tpu as pltpu
from jax.sharding import PartitionSpec as P

MESH = pl.DeviceIdType.MESH
BF = jnp.bfloat16
F32 = jnp.float32
COLS = 256
NT = 10
NJ = 5
ROWS = 320
SEQ = 256
HALF = 1280


def span(start, size):
    return pl.ds(pl.multiple_of(start, size), size)


def kernel(level, rate_ref, x_hbm, t_hbm, m_hbm, w_hbm, mom_hbm, neww_hbm, newm_hbm,
           win, wb, mom, xk, xt, tk, mk, wk, ps, pr, rb, gb, go, gr, hs, gh, ga, hb, gbuf, rel,
           ld, xs, xr, xos, xor_, ts, tr, ms, mr, ws, wr, wss, wsr, pss, psr, rs, rr,
           gs, grr, hss, hsr, as_, ar, bs, br, outs):
    r = lax.axis_index("replica")
    f = lax.axis_index("fsdp")
    c = lax.rem(r, 2)
    pair = r - c
    yh = f // 4
    x = lax.rem(f, 4)
    lo = lax.rem(x, 2)
    hi = x // 2
    xo = x + 1 - 2 * lo
    across = 3 - x
    o = lax.rem(lo + hi, 2)
    home = c == yh
    away = jnp.logical_not(home)

    def dev(core, y, xx):
        return (pair + core, y * 4 + xx)

    def other(offset):
        return (lax.rem(r + offset, 32), f)

    partner = dev(1 - c, yh, x)
    worker = dev(yh, c, x)
    worker_o = dev(yh, c, xo)
    side_o = dev(c, yh, xo)
    side_s = dev(c, yh, across)

    def remote(src, dst, ss, rsem, to):
        return pltpu.make_async_remote_copy(src_ref=src, dst_ref=dst, send_sem=ss, recv_sem=rsem,
                                            device_id=to, device_id_type=MESH)

    def arrived(dst, rsem, site=None):
        remote(dst, dst, rsem, rsem, partner).wait_recv()

    def local_or_remote(src, dst, ss, rsem):
        @pl.when(home)
        def _():
            pltpu.make_async_copy(src, dst, rsem).start()

        @pl.when(away)
        def _():
            remote(src, dst, ss, rsem, worker).start()

    def w_load(t):
        return pltpu.make_async_copy(w_hbm.at[:, span(t * COLS, COLS)], win.at[t], ld.at[t])

    @pl.loop(0, NJ)
    def _(j):
        w_load(o * NJ + j).start()

    @pl.loop(0, NJ)
    def _(j):
        w_load((1 - o) * NJ + j).start()

    m_load = pltpu.make_async_copy(mom_hbm, mom, ld.at[NT])
    m_load.start()

    near, later = 2**level, 2 ** ((level + 1) % 5)
    if level == 1:
        near, later = later, near
    if level == 3:
        offsets = [8, 16, 24]
    elif level == 0:
        offsets = [1, 2, 3, 29, 30, 31]
    else:
        offsets = sorted({near, 32 - near, later, 32 - later})
    if level == 2:
        offsets += [12, 20]
    barrier = pltpu.get_barrier_semaphore()
    peers = [partner, dev(c, 1 - yh, x), dev(1 - c, 1 - yh, x), side_s]
    peers += [dev(a, b, xo) for a in (0, 1) for b in (0, 1)]
    peers += [other(a) for a in offsets]
    for peer in peers:
        pl.semaphore_signal(barrier, inc=1, device_id=peer, device_id_type=MESH)
    pl.semaphore_wait(barrier, len(peers))

    def x_send(k):
        return remote(x_hbm.at[:, span(k * HALF, HALF)], xk.at[yh * 2 + lo], xs.at[k], xr.at[yh], dev(k, c, x))

    @pl.loop(0, 2)
    def _(k):
        mine = jnp.logical_and(home, c == k)

        @pl.when(mine)
        def _():
            pltpu.make_async_copy(x_hbm.at[:, span(k * HALF, HALF)], xk.at[yh * 2 + lo], xr.at[yh]).start()

        @pl.when(jnp.logical_not(mine))
        def _():
            x_send(k).start()

    def own_rows(j):
        return wk.at[j, span(x * ROWS, ROWS)]

    def o_rows(j):
        return wk.at[j, span(xo * ROWS, ROWS)]

    def w_keep(j):
        return remote(wb.at[o * NJ + j], own_rows(j), ws.at[0, j], wr.at[lo, j], worker)

    def w_give(j):
        return remote(wb.at[(1 - o) * NJ + j], own_rows(j), ws.at[1, j], wr.at[lo, j], worker_o)

    def w_own_on(src, j):
        return remote(src, own_rows(j), wss.at[0, j], wsr.at[lo, j], side_s)

    def w_o_on(j):
        return remote(o_rows(j), o_rows(j), wss.at[1, j], wsr.at[1 - lo, j], side_s)

    def cast(t):
        w_load(t).wait()
        wb[t] = win[t].astype(BF)

    def t_cols(side, j):
        half = o if side == 0 else 1 - o
        return t_hbm.at[:, span(half * HALF + j * COLS, COLS)]

    t_dst = span(lo * SEQ, SEQ)

    def t_keep(j):
        return remote(t_cols(0, j), tk.at[j, t_dst], ts.at[0, j], tr.at[lo, j], worker)

    def t_give(j):
        return remote(t_cols(1, j), tk.at[j, t_dst], ts.at[1, j], tr.at[lo, j], worker_o)

    m_dst = mk.at[span(lo * SEQ, SEQ)]
    m_keep = remote(m_hbm, m_dst, ms.at[0], mr.at[lo], worker)
    m_give = remote(m_hbm, m_dst, ms.at[1], mr.at[lo], worker_o)

    @pl.loop(0, NJ)
    def _(j):
        t = o * NJ + j
        cast(t)

        @pl.when(home)
        def _():
            pltpu.make_async_copy(wb.at[t], own_rows(j), wr.at[lo, j]).start()
            w_own_on(wb.at[t], j).start()
            pltpu.make_async_copy(t_cols(0, j), tk.at[j, t_dst], tr.at[lo, j]).start()

        @pl.when(away)
        def _():
            w_keep(j).start()

    def turn(slot):
        xt[:, span(slot * SEQ, SEQ)] = xk[slot].T

    def x_on(ry):
        slot = ry * 2 + lo
        return remote(xk.at[slot], xk.at[slot], xos.at[ry], xor_.at[ry], side_o)

    arrived(xk.at[yh * 2 + lo], xr.at[yh], 0)
    x_on(yh).start()

    def give_t(j):
        t_give(j).start()

        @pl.when(away)
        def _():
            t_keep(j).start()

    def give(j):
        @pl.when(j < NJ)
        def _():
            w_give(j).start()

        @pl.when(j >= 2)
        def _():
            give_t(j - 1)

    cast((1 - o) * NJ)

    @pl.when(home)
    def _():
        w_give(0).start()
        m_give.start()
        give_t(0)
        pltpu.make_async_copy(m_hbm, m_dst, mr.at[lo]).start()

    @pl.loop(1, NJ)
    def _(j):
        cast((1 - o) * NJ + j)

    if level == 3:
        member = r // 8
        quarter = ROWS // 4

        def part(q):
            return span(q * quarter, quarter)

        def a_copy(d):
            q = lax.rem(member + d, 4)
            return remote(wb.at[:, part(q)], ga.at[:, part(d - 1)], as_.at[d - 1], ar.at[d - 1], other(8 * d))

        def b_copy(d):
            return remote(hb.at[:, part(member)], hb.at[:, part(member)], bs.at[d - 1], br.at[d - 1], other(8 * d))

        first_copies, second_copies = (1, 4), (1, 4)
    else:
        first = 1 + 2 * c if level == 0 else near

        def a_copy(t):
            return remote(wb.at[t], ga.at[t], as_.at[t], ar.at[t], other(first))

        def pass_on(t):
            return remote(gbuf.at[t], gbuf.at[t], as_.at[NT + t], br.at[t], partner)

        def b_copy(t):
            return remote(hb.at[t], gbuf.at[t], bs.at[t], br.at[t], other(later))

        def leg(k):
            return remote(hb.at[k * NJ], rel.at[k], bs.at[k * NJ], ar.at[NT + k], other(20))

        def next_leg(k):
            return remote(rel.at[k], gbuf.at[k * NJ], as_.at[NT + k], br.at[k * NJ], other(20))

        first_copies, second_copies = (0, NT), (0, NT)

    def order(t):
        return lax.rem(t, 2) * NJ + t // 2

    def first_transfer():
        @pl.loop(*first_copies)
        def _(t):
            a_copy(t if level == 3 else order(t)).start()

    first_transfer()
    turn(yh * 2 + lo)
    arrived(xk.at[(1 - yh) * 2 + lo], xr.at[1 - yh], 1)
    x_on(1 - yh).start()

    @pl.when(home)
    def _():
        pl.loop(1, NJ + 1)(give)

    @pl.when(away)
    def _():
        w_give(0).start()
        give_t(0)
        m_keep.start()
        m_give.start()

    turn((1 - yh) * 2 + lo)

    def gossip_half(n):
        t = order(n)
        arrived(ga.at[t], ar.at[t], 40 + t)

        @pl.loop(0, 5)
        def _(i):
            rows = span(i * 64, 64)
            half = (win[t, rows] + ga[t, rows].astype(F32)) * 0.5
            win[t, rows] = half
            hb[t, rows] = half.astype(BF)

        if level == 0:
            pl.when(c == 1)(b_copy(t).start)
        elif level == 1:
            pl.when(n >= 4)(b_copy(t).start)
        elif level == 2:
            pl.when(n < 2)(leg(lax.min(n, 1)).start)
            pl.when(n >= 2)(b_copy(t).start)
        else:
            b_copy(t).start()

    def gossip_quarter():
        for d in range(3):
            arrived(ga.at[:, part(d)], ar.at[d], 40 + d)

        @pl.loop(0, NT)
        def _(t):
            total = win[t, part(member)]
            for d in range(3):
                total += ga[t, part(d)].astype(F32)
            hb[t, part(member)] = (total * 0.25).astype(BF)

        @pl.loop(*second_copies)
        def _(d):
            b_copy(d).start()

    def forward(j):
        arrived(o_rows(j), wr.at[1 - lo, j], 50 + j)
        w_o_on(j).start()

    @pl.when(away)
    def _():
        @pl.loop(0, NJ)
        def _(j):
            arrived(own_rows(j), wr.at[lo, j], 2)
            w_own_on(own_rows(j), j).start()

        pl.loop(1, NJ + 1)(give)

    arrived(xk.at[yh * 2 + 1 - lo], xor_.at[yh], 3)
    turn(yh * 2 + 1 - lo)
    if level in (1, 2):

        @pl.loop(0, 4)
        def _(t):
            gossip_half(t)

    forward(0)
    arrived(xk.at[(1 - yh) * 2 + 1 - lo], xor_.at[1 - yh], 4)

    def p_copy(j):
        return remote(ps.at[j, span((1 - c) * 512, 512)], pr.at[j], pss.at[j], psr.at[j], partner)

    def step_p(j):
        @pl.when(home)
        def _():
            arrived(own_rows(j), wr.at[lo, j], 5)

        arrived(wk.at[j, span(across * ROWS, ROWS)], wsr.at[1 - lo, j], 60 + j)
        arrived(wk.at[j, span((3 - xo) * ROWS, ROWS)], wsr.at[lo, j], 70 + j)

        @pl.loop(0, 4)
        def _(i):
            b = lax.rem((1 - c) * 2 + i, 4)
            ps[j, span(b * SEQ, SEQ)] = jnp.dot(xk[b], wk[j], preferred_element_type=F32)

            @pl.when(i == 1)
            def _():
                p_copy(j).start()

    def r_copy(j):
        ref = rb.at[j, span(c * 512, 512)]
        return remote(ref, ref, rs.at[j], rr.at[j], partner)

    def step_r(j):
        @pl.when(j == 0)
        def _():
            for side in range(2):
                arrived(mk.at[pl.ds(side * SEQ, SEQ)], mr.at[side], 6)

        arrived(tk.at[j, span(lo * SEQ, SEQ)], tr.at[lo, j], 80 + j)
        arrived(tk.at[j, span((1 - lo) * SEQ, SEQ)], tr.at[1 - lo, j], 80 + j)
        arrived(pr.at[j], psr.at[j], 90 + j)

        @pl.loop(0, 8)
        def _(i):
            rows = span(i * 64, 64)
            full = span(c * 512 + i * 64, 64)
            scale = mk[rows].astype(F32)
            scale = jnp.concatenate([scale, scale], axis=1)
            pred = ps[j, full] + pr[j, rows]
            rb[j, full] = (scale * (pred - tk[j, rows].astype(F32))).astype(BF)

        r_copy(j).start()

    def g_copy(j, side):
        rows = span(side * ROWS, ROWS)
        return remote(gb.at[j, rows], gr.at[j, rows], gs.at[side, j], grr.at[side, j], side_s)

    def step_g(j):
        arrived(rb.at[j, span((1 - c) * 512, 512)], rr.at[j], 100 + j)

        @pl.loop(0, 4)
        def _(i):
            half = jnp.where(i < 2, 1 - hi, hi)
            side = lax.rem(lo + i, 2)
            value = jnp.dot(xt[span((half * 2 + side) * ROWS, ROWS)], rb[j], preferred_element_type=F32)
            rows = span(side * ROWS, ROWS)

            @pl.when(i < 2)
            def _():
                gb[j, rows] = value.astype(BF)
                pl.when(away)(g_copy(j, side).start)

            @pl.when(i >= 2)
            def _():
                go[j, rows] = value

    def h_give(j):
        return remote(hs.at[j, span((1 - lo) * ROWS, ROWS)], gh.at[o * NJ + j], hss.at[1, j], hsr.at[o * NJ + j], worker_o)

    def h_keep(j):
        return remote(hs.at[j, span(lo * ROWS, ROWS)], gh.at[o * NJ + j], hss.at[0, j], hsr.at[o * NJ + j], worker)

    def step_h(j):
        @pl.loop(0, 2)
        def _(i):
            side = lax.rem(1 - lo + i, 2)
            arrived(gr.at[j, span(side * ROWS, ROWS)], grr.at[side, j], 110 + j)

            @pl.loop(0, 5)
            def _(k):
                rows = span(side * ROWS + k * 64, 64)
                hs[j, rows] = (go[j, rows] + gr[j, rows].astype(F32)).astype(BF)

            @pl.when(i == 0)
            def _():
                h_give(j).start()

        local_or_remote(hs.at[j, span(lo * ROWS, ROWS)], gh.at[o * NJ + j], hss.at[0, j], hsr.at[o * NJ + j])

    rate = rate_ref[0]

    def out_w(t):
        return pltpu.make_async_copy(win.at[t], neww_hbm.at[:, span(t * COLS, COLS)], outs.at[0, t])

    def out_m(t):
        cols = span(t * COLS, COLS)
        return pltpu.make_async_copy(mom.at[:, cols], newm_hbm.at[:, cols], outs.at[1, t])

    def finish(t):
        arrived(gh.at[t], hsr.at[t], 120 + t)
        if level == 0:
            pl.when(c == 0)(functools.partial(arrived, gbuf.at[t], br.at[t], 130))
        elif level != 3:
            arrived(gbuf.at[t], br.at[t], 130 + t)

        @pl.loop(0, 5)
        def _(i):
            rows = span(i * 64, 64)
            cols = span(t * COLS, COLS)
            moved = (0.9 * mom[rows, cols].astype(F32) + gh[t, rows].astype(F32)).astype(BF)
            mom[rows, cols] = moved
            if level == 3:
                mixed = hb[t, rows].astype(F32)
            else:
                mixed = (win[t, rows] + gbuf[t, rows].astype(F32)) * 0.5
            win[t, rows] = mixed - rate * moved.astype(F32)

        out_w(t).start()
        out_m(t).start()

    @pl.loop(0, NJ + 4)
    def _(i):
        pl.when(i < NJ)(functools.partial(step_p, i))

        @pl.when(jnp.logical_and(home, jnp.logical_and(i >= 1, i <= NJ)))
        def _():
            g_copy(i - 1, lo).start()
            g_copy(i - 1, 1 - lo).start()

        @pl.when(i < NJ)
        def _():

            @pl.when(i == 0)
            def _():
                turn((1 - yh) * 2 + 1 - lo)
                if level == 1:

                    @pl.loop(0, 4)
                    def _(t):
                        b_copy(order(t)).start()

                forward(1)

            step_r(i)

            @pl.when(i < NJ - 2)
            def _():
                forward(i + 2)

            step_g(i)

        @pl.when(jnp.logical_and(i >= 2, i < NJ + 2))
        def _():
            step_h(i - 2)

        if level == 3:

            @pl.when(i == 1)
            def _():
                gossip_quarter()
        elif level == 0:

            @pl.when(i < 2)
            def _():
                @pl.loop(5 * i, 5 * i + 5)
                def _(t):
                    gossip_half(t)

            @pl.when(jnp.logical_and(i == 3, c == 1))
            def _():
                @pl.loop(0, NT)
                def _(t):
                    arrived(gbuf.at[t], br.at[t], 140)
                    pass_on(t).start()
        elif level in (1, 2):

            @pl.when(i < 2)
            def _():
                @pl.loop(4 + 3 * i, 7 + 3 * i)
                def _(t):
                    gossip_half(t)

            if level == 2:

                @pl.when(i == 2)
                def _():
                    for k in range(2):
                        arrived(rel.at[k], ar.at[NT + k], 141 + k)
                        next_leg(k).start()
        else:

            @pl.when(i < 5)
            def _():
                @pl.loop(2 * i, 2 * i + 2)
                def _(t):
                    gossip_half(t)

        @pl.when(i == 4)
        def _():
            m_load.wait()
            if level == 3:
                for d in range(1, 4):
                    arrived(hb.at[:, part(lax.rem(member + 4 - d, 4))], br.at[d - 1], 130)

        @pl.when(i >= 4)
        def _():
            @pl.loop(0, 2)
            def _(h):
                finish(h * NJ + i - 4)

    @pl.loop(0, 2)
    def _(k):
        @pl.when(jnp.logical_not(jnp.logical_and(home, c == k)))
        def _():
            x_send(k).wait_send()

        x_on(k).wait_send()

    m_give.wait_send()
    pl.when(away)(m_keep.wait_send)

    @pl.loop(0, NJ)
    def _(j):
        @pl.when(away)
        def _():
            w_keep(j).wait_send()
            t_keep(j).wait_send()
            h_keep(j).wait_send()

        for copy in (w_give(j), t_give(j), h_give(j), w_own_on(own_rows(j), j), w_o_on(j), p_copy(j), r_copy(j),
                     g_copy(j, 0), g_copy(j, 1)):
            copy.wait_send()

    @pl.loop(*first_copies)
    def _(t):
        a_copy(t).wait_send()

    if level == 0:

        @pl.when(c == 1)
        def _():
            @pl.loop(0, NT)
            def _(t):
                b_copy(t).wait_send()
                pass_on(t).wait_send()
    else:

        @pl.loop(*second_copies)
        def _(t):
            b_copy(t).wait_send()

        if level == 2:
            for k in range(2):
                next_leg(k).wait_send()

    @pl.loop(0, NT)
    def _(t):
        out_w(t).wait()
        out_m(t).wait()


def update(level, rate, tokens, goals, marks, shard, momentum):
    dma = pltpu.SemaphoreType.DMA
    anywhere = pl.BlockSpec(memory_space=pl.ANY)
    vm = pltpu.VMEM
    return pl.pallas_call(
        functools.partial(kernel, level),
        out_shape=(
            jax.ShapeDtypeStruct((ROWS, NT * COLS), F32),
            jax.ShapeDtypeStruct((ROWS, NT * COLS), BF),
        ),
        in_specs=[pl.BlockSpec(memory_space=pltpu.SMEM)] + [anywhere] * 5,
        out_specs=(anywhere, anywhere),
        scratch_shapes=[
            vm((NT, ROWS, COLS), F32),
            vm((NT, ROWS, COLS), BF),
            vm((ROWS, NT * COLS), BF),
            vm((4, SEQ, HALF), BF),
            vm((HALF, 4 * SEQ), BF),
            vm((NJ, 2 * SEQ, COLS), BF),
            vm((2 * SEQ, 128), BF),
            vm((NJ, HALF, COLS), BF),
            vm((NJ, 4 * SEQ, COLS), F32),
            vm((NJ, 2 * SEQ, COLS), F32),
            vm((NJ, 4 * SEQ, COLS), BF),
            vm((NJ, 2 * ROWS, COLS), BF),
            vm((NJ, 2 * ROWS, COLS), F32),
            vm((NJ, 2 * ROWS, COLS), BF),
            vm((NJ, 2 * ROWS, COLS), BF),
            vm((NT, ROWS, COLS), BF),
            vm((NT, ROWS, COLS), BF),
            vm((NT, ROWS, COLS), BF),
            vm((NT, ROWS, COLS), BF),
            vm((2, ROWS, COLS), BF),
            dma((NT + 1,)),
            dma((2,)), dma((2,)),
            dma((2,)), dma((2,)),
            dma((2, NJ)), dma((2, NJ)),
            dma((2,)), dma((2,)),
            dma((2, NJ)), dma((2, NJ)),
            dma((2, NJ)), dma((2, NJ)),
            dma((NJ,)), dma((NJ,)),
            dma((NJ,)), dma((NJ,)),
            dma((2, NJ)), dma((2, NJ)),
            dma((2, NJ)), dma((NT,)),
            dma((2 * NT,)), dma((2 * NT,)),
            dma((NT,)), dma((NT,)),
            dma((2, NT)),
        ],
        compiler_params=pltpu.CompilerParams(
            collective_id=level, has_side_effects=True, vmem_limit_bytes=60 * 2**20
        ),
        name=f"update_{level}",
    )(rate, tokens, goals, marks, shard, momentum)


def local(inputs, targets, masked, step_index, weights, momentum):
    marks = jnp.broadcast_to((masked[0].astype(F32) / 2048.0).astype(BF)[:, None], (SEQ, 128))
    rate = ((step_index.astype(F32) + 1.0) / 500.0).reshape(1)
    branches = [functools.partial(update, level) for level in range(5)]
    new_weights, new_momentum = lax.switch(
        step_index % 5, branches, rate, inputs[0], targets[0], marks, weights[0], momentum[0]
    )
    return new_weights[None], new_momentum[None]


def solution(mesh):
    in_specs = (
        P("replica", "fsdp", None),
        P("replica", "fsdp", None),
        P("replica", "fsdp"),
        P(),
        P("replica", "fsdp", None),
        P("replica", "fsdp", None),
    )
    out_specs = (P("replica", "fsdp", None), P("replica", "fsdp", None))
    return jax.shard_map(local, mesh=mesh, in_specs=in_specs, out_specs=out_specs, check_vma=False)
```

```python
import functools

import jax
import jax.numpy as jnp
from jax import lax
from jax.experimental import pallas as pl
from jax.experimental.pallas import tpu as pltpu
from jax.sharding import PartitionSpec as P

MESH = pl.DeviceIdType.MESH
BF = jnp.bfloat16
F32 = jnp.float32
COLS = 256
NT = 10
NJ = 5
ROWS = 320
SEQ = 256
HALF = 1280


def span(start, size):
    return pl.ds(pl.multiple_of(start, size), size)


def kernel(level, rate_ref, x_hbm, t_hbm, m_hbm, w_hbm, mom_hbm, neww_hbm, newm_hbm,
           win, wb, mom, xk, xt, tk, mk, wk, ps, pb, pr, rb, gb, go, gr, hs, gh, ga, hb, gbuf, rel,
           ld, xs, xr, xos, xor_, ts, tr, ms, mr, ws, wr, wss, wsr, pss, psr, rs, rr,
           gs, grr, hss, hsr, as_, ar, bs, br, outs):
    r = lax.axis_index("replica")
    f = lax.axis_index("fsdp")
    c = lax.rem(r, 2)
    pair = r - c
    yh = f // 4
    x = lax.rem(f, 4)
    lo = lax.rem(x, 2)
    hi = x // 2
    xo = x + 1 - 2 * lo
    across = 3 - x
    o = lax.rem(lo + hi, 2)
    home = c == yh
    away = jnp.logical_not(home)

    def dev(core, y, xx):
        return (pair + core, y * 4 + xx)

    def other(offset):
        return (lax.rem(r + offset, 32), f)

    partner = dev(1 - c, yh, x)
    worker = dev(yh, c, x)
    worker_o = dev(yh, c, xo)
    side_o = dev(c, yh, xo)
    side_s = dev(c, yh, across)

    def remote(src, dst, ss, rsem, to):
        return pltpu.make_async_remote_copy(src_ref=src, dst_ref=dst, send_sem=ss, recv_sem=rsem,
                                            device_id=to, device_id_type=MESH)

    def arrived(dst, rsem, site=None):
        remote(dst, dst, rsem, rsem, partner).wait_recv()

    def local_or_remote(src, dst, ss, rsem):
        @pl.when(home)
        def _():
            pltpu.make_async_copy(src, dst, rsem).start()

        @pl.when(away)
        def _():
            remote(src, dst, ss, rsem, worker).start()

    def w_load(t):
        return pltpu.make_async_copy(w_hbm.at[:, span(t * COLS, COLS)], win.at[t], ld.at[t])

    @pl.loop(0, NJ)
    def _(j):
        w_load(o * NJ + j).start()

    @pl.loop(0, NJ)
    def _(j):
        w_load((1 - o) * NJ + j).start()

    m_load = pltpu.make_async_copy(mom_hbm, mom, ld.at[NT])
    m_load.start()

    near, later = 2**level, 2 ** ((level + 1) % 5)
    if level == 1:
        near, later = later, near
    if level == 3:
        offsets = [8, 16, 24]
    elif level == 0:
        offsets = [1, 2, 3, 29, 30, 31]
    else:
        offsets = sorted({near, 32 - near, later, 32 - later})
    if level == 2:
        offsets += [12, 20]
    barrier = pltpu.get_barrier_semaphore()
    peers = [partner, dev(c, 1 - yh, x), dev(1 - c, 1 - yh, x), side_s]
    peers += [dev(a, b, xo) for a in (0, 1) for b in (0, 1)]
    peers += [other(a) for a in offsets]
    for peer in peers:
        pl.semaphore_signal(barrier, inc=1, device_id=peer, device_id_type=MESH)
    pl.semaphore_wait(barrier, len(peers))

    def x_send(k):
        return remote(x_hbm.at[:, span(k * HALF, HALF)], xk.at[yh * 2 + lo], xs.at[k], xr.at[yh], dev(k, c, x))

    @pl.loop(0, 2)
    def _(k):
        mine = jnp.logical_and(home, c == k)

        @pl.when(mine)
        def _():
            pltpu.make_async_copy(x_hbm.at[:, span(k * HALF, HALF)], xk.at[yh * 2 + lo], xr.at[yh]).start()

        @pl.when(jnp.logical_not(mine))
        def _():
            x_send(k).start()

    def own_rows(j):
        return wk.at[j, span(x * ROWS, ROWS)]

    def o_rows(j):
        return wk.at[j, span(xo * ROWS, ROWS)]

    def w_keep(j):
        return remote(wb.at[o * NJ + j], own_rows(j), ws.at[0, j], wr.at[lo, j], worker)

    def w_give(j):
        return remote(wb.at[(1 - o) * NJ + j], own_rows(j), ws.at[1, j], wr.at[lo, j], worker_o)

    def w_own_on(src, j):
        return remote(src, own_rows(j), wss.at[0, j], wsr.at[lo, j], side_s)

    def w_o_on(j):
        return remote(o_rows(j), o_rows(j), wss.at[1, j], wsr.at[1 - lo, j], side_s)

    def cast(t):
        w_load(t).wait()
        wb[t] = win[t].astype(BF)

    def t_cols(side, j):
        half = o if side == 0 else 1 - o
        return t_hbm.at[:, span(half * HALF + j * COLS, COLS)]

    t_dst = span(lo * SEQ, SEQ)

    def t_keep(j):
        return remote(t_cols(0, j), tk.at[j, t_dst], ts.at[0, j], tr.at[lo, j], worker)

    def t_give(j):
        return remote(t_cols(1, j), tk.at[j, t_dst], ts.at[1, j], tr.at[lo, j], worker_o)

    m_dst = mk.at[span(lo * SEQ, SEQ)]
    m_keep = remote(m_hbm, m_dst, ms.at[0], mr.at[lo], worker)
    m_give = remote(m_hbm, m_dst, ms.at[1], mr.at[lo], worker_o)

    @pl.loop(0, NJ)
    def _(j):
        t = o * NJ + j
        cast(t)

        @pl.when(home)
        def _():
            pltpu.make_async_copy(wb.at[t], own_rows(j), wr.at[lo, j]).start()
            w_own_on(wb.at[t], j).start()
            pltpu.make_async_copy(t_cols(0, j), tk.at[j, t_dst], tr.at[lo, j]).start()

        @pl.when(away)
        def _():
            w_keep(j).start()

    def turn(slot):
        xt[:, span(slot * SEQ, SEQ)] = xk[slot].T

    def x_on(ry):
        slot = ry * 2 + lo
        return remote(xk.at[slot], xk.at[slot], xos.at[ry], xor_.at[ry], side_o)

    arrived(xk.at[yh * 2 + lo], xr.at[yh], 0)
    x_on(yh).start()

    def give_t(j):
        t_give(j).start()

        @pl.when(away)
        def _():
            t_keep(j).start()

    def give(j):
        @pl.when(j < NJ)
        def _():
            w_give(j).start()

        @pl.when(j >= 2)
        def _():
            give_t(j - 1)

    cast((1 - o) * NJ)

    @pl.when(home)
    def _():
        w_give(0).start()
        m_give.start()
        give_t(0)
        pltpu.make_async_copy(m_hbm, m_dst, mr.at[lo]).start()

    @pl.loop(1, NJ)
    def _(j):
        cast((1 - o) * NJ + j)

    if level == 3:
        member = r // 8
        quarter = ROWS // 4

        def part(q):
            return span(q * quarter, quarter)

        def a_copy(d):
            q = lax.rem(member + d, 4)
            return remote(wb.at[:, part(q)], ga.at[:, part(d - 1)], as_.at[d - 1], ar.at[d - 1], other(8 * d))

        def b_copy(d):
            return remote(hb.at[:, part(member)], hb.at[:, part(member)], bs.at[d - 1], br.at[d - 1], other(8 * d))

        first_copies, second_copies = (1, 4), (1, 4)
    else:
        first = 1 + 2 * c if level == 0 else near

        def a_copy(t):
            return remote(wb.at[t], ga.at[t], as_.at[t], ar.at[t], other(first))

        def pass_on(t):
            return remote(gbuf.at[t], gbuf.at[t], as_.at[NT + t], br.at[t], partner)

        def b_copy(t):
            return remote(hb.at[t], gbuf.at[t], bs.at[t], br.at[t], other(later))

        def leg(k):
            return remote(hb.at[k * NJ], rel.at[k], bs.at[k * NJ], ar.at[NT + k], other(20))

        def next_leg(k):
            return remote(rel.at[k], gbuf.at[k * NJ], as_.at[NT + k], br.at[k * NJ], other(20))

        first_copies, second_copies = (0, NT), (0, NT)

    def order(t):
        return lax.rem(t, 2) * NJ + t // 2

    def first_transfer():
        @pl.loop(*first_copies)
        def _(t):
            a_copy(t if level == 3 else order(t)).start()

    first_transfer()
    turn(yh * 2 + lo)
    arrived(xk.at[(1 - yh) * 2 + lo], xr.at[1 - yh], 1)
    x_on(1 - yh).start()

    @pl.when(home)
    def _():
        pl.loop(1, NJ + 1)(give)

    @pl.when(away)
    def _():
        w_give(0).start()
        give_t(0)
        m_keep.start()
        m_give.start()

    turn((1 - yh) * 2 + lo)

    def gossip_half(n):
        t = order(n)
        arrived(ga.at[t], ar.at[t], 40 + t)

        @pl.loop(0, 5)
        def _(i):
            rows = span(i * 64, 64)
            half = (win[t, rows] + ga[t, rows].astype(F32)) * 0.5
            win[t, rows] = half
            hb[t, rows] = half.astype(BF)

        if level == 0:
            pl.when(c == 1)(b_copy(t).start)
        elif level == 1:
            pl.when(n >= 4)(b_copy(t).start)
        elif level == 2:
            pl.when(n < 2)(leg(lax.min(n, 1)).start)
            pl.when(n >= 2)(b_copy(t).start)
        else:
            b_copy(t).start()

    def gossip_quarter():
        for d in range(3):
            arrived(ga.at[:, part(d)], ar.at[d], 40 + d)

        @pl.loop(0, NT)
        def _(t):
            total = win[t, part(member)]
            for d in range(3):
                total += ga[t, part(d)].astype(F32)
            hb[t, part(member)] = (total * 0.25).astype(BF)

        @pl.loop(*second_copies)
        def _(d):
            b_copy(d).start()

    def forward(j):
        arrived(o_rows(j), wr.at[1 - lo, j], 50 + j)
        w_o_on(j).start()

    @pl.when(away)
    def _():
        @pl.loop(0, NJ)
        def _(j):
            arrived(own_rows(j), wr.at[lo, j], 2)
            w_own_on(own_rows(j), j).start()

        pl.loop(1, NJ + 1)(give)

    arrived(xk.at[yh * 2 + 1 - lo], xor_.at[yh], 3)
    turn(yh * 2 + 1 - lo)
    if level in (1, 2):

        @pl.loop(0, 4)
        def _(t):
            gossip_half(t)

    forward(0)
    arrived(xk.at[(1 - yh) * 2 + 1 - lo], xor_.at[1 - yh], 4)

    def p_copy(j):
        return remote(pb.at[j], pr.at[j], pss.at[j], psr.at[j], partner)

    def step_p(j):
        @pl.when(home)
        def _():
            arrived(own_rows(j), wr.at[lo, j], 5)

        arrived(wk.at[j, span(across * ROWS, ROWS)], wsr.at[1 - lo, j], 60 + j)
        arrived(wk.at[j, span((3 - xo) * ROWS, ROWS)], wsr.at[lo, j], 70 + j)

        @pl.loop(0, 4)
        def _(i):
            b = lax.rem((1 - c) * 2 + i, 4)
            value = jnp.dot(xk[b], wk[j], preferred_element_type=F32)
            rows = span(lax.rem(i, 2) * SEQ, SEQ)

            @pl.when(i < 2)
            def _():
                pb[j, rows] = value.astype(BF)

            @pl.when(i >= 2)
            def _():
                ps[j, rows] = value

            @pl.when(i == 1)
            def _():
                p_copy(j).start()

    def r_copy(j):
        ref = rb.at[j, span(c * 512, 512)]
        return remote(ref, ref, rs.at[j], rr.at[j], partner)

    def step_r(j):
        @pl.when(j == 0)
        def _():
            for side in range(2):
                arrived(mk.at[pl.ds(side * SEQ, SEQ)], mr.at[side], 6)

        arrived(tk.at[j, span(lo * SEQ, SEQ)], tr.at[lo, j], 80 + j)
        arrived(tk.at[j, span((1 - lo) * SEQ, SEQ)], tr.at[1 - lo, j], 80 + j)
        arrived(pr.at[j], psr.at[j], 90 + j)

        @pl.loop(0, 8)
        def _(i):
            rows = span(i * 64, 64)
            full = span(c * 512 + i * 64, 64)
            scale = mk[rows].astype(F32)
            scale = jnp.concatenate([scale, scale], axis=1)
            pred = ps[j, rows] + pr[j, rows].astype(F32)
            rb[j, full] = (scale * (pred - tk[j, rows].astype(F32))).astype(BF)

        r_copy(j).start()

    def g_copy(j, side):
        rows = span(side * ROWS, ROWS)
        return remote(gb.at[j, rows], gr.at[j, rows], gs.at[side, j], grr.at[side, j], side_s)

    def step_g(j):
        arrived(rb.at[j, span((1 - c) * 512, 512)], rr.at[j], 100 + j)

        @pl.loop(0, 4)
        def _(i):
            half = jnp.where(i < 2, 1 - hi, hi)
            side = lax.rem(lo + i, 2)
            value = jnp.dot(xt[span((half * 2 + side) * ROWS, ROWS)], rb[j], preferred_element_type=F32)
            rows = span(side * ROWS, ROWS)

            @pl.when(i < 2)
            def _():
                gb[j, rows] = value.astype(BF)
                pl.when(away)(g_copy(j, side).start)

            @pl.when(i >= 2)
            def _():
                go[j, rows] = value

    def h_give(j):
        return remote(hs.at[j, span((1 - lo) * ROWS, ROWS)], gh.at[o * NJ + j], hss.at[1, j], hsr.at[o * NJ + j], worker_o)

    def h_keep(j):
        return remote(hs.at[j, span(lo * ROWS, ROWS)], gh.at[o * NJ + j], hss.at[0, j], hsr.at[o * NJ + j], worker)

    def step_h(j):
        @pl.loop(0, 2)
        def _(i):
            side = lax.rem(1 - lo + i, 2)
            arrived(gr.at[j, span(side * ROWS, ROWS)], grr.at[side, j], 110 + j)

            @pl.loop(0, 5)
            def _(k):
                rows = span(side * ROWS + k * 64, 64)
                hs[j, rows] = (go[j, rows] + gr[j, rows].astype(F32)).astype(BF)

            @pl.when(i == 0)
            def _():
                h_give(j).start()

        local_or_remote(hs.at[j, span(lo * ROWS, ROWS)], gh.at[o * NJ + j], hss.at[0, j], hsr.at[o * NJ + j])

    rate = rate_ref[0]

    def out_w(t):
        return pltpu.make_async_copy(win.at[t], neww_hbm.at[:, span(t * COLS, COLS)], outs.at[0, t])

    def out_m(t):
        cols = span(t * COLS, COLS)
        return pltpu.make_async_copy(mom.at[:, cols], newm_hbm.at[:, cols], outs.at[1, t])

    def finish(t):
        arrived(gh.at[t], hsr.at[t], 120 + t)
        if level == 0:
            pl.when(c == 0)(functools.partial(arrived, gbuf.at[t], br.at[t], 130))
        elif level != 3:
            arrived(gbuf.at[t], br.at[t], 130 + t)

        @pl.loop(0, 5)
        def _(i):
            rows = span(i * 64, 64)
            cols = span(t * COLS, COLS)
            moved = (0.9 * mom[rows, cols].astype(F32) + gh[t, rows].astype(F32)).astype(BF)
            mom[rows, cols] = moved
            if level == 3:
                mixed = hb[t, rows].astype(F32)
            else:
                mixed = (win[t, rows] + gbuf[t, rows].astype(F32)) * 0.5
            win[t, rows] = mixed - rate * moved.astype(F32)

        out_w(t).start()
        out_m(t).start()

    @pl.loop(0, NJ + 4)
    def _(i):
        pl.when(i < NJ)(functools.partial(step_p, i))

        @pl.when(jnp.logical_and(home, jnp.logical_and(i >= 1, i <= NJ)))
        def _():
            g_copy(i - 1, lo).start()
            g_copy(i - 1, 1 - lo).start()

        @pl.when(i < NJ)
        def _():

            @pl.when(i == 0)
            def _():
                turn((1 - yh) * 2 + 1 - lo)
                if level == 1:

                    @pl.loop(0, 4)
                    def _(t):
                        b_copy(order(t)).start()

                forward(1)

            step_r(i)

            @pl.when(i < NJ - 2)
            def _():
                forward(i + 2)

            step_g(i)

        @pl.when(jnp.logical_and(i >= 2, i < NJ + 2))
        def _():
            step_h(i - 2)

        if level == 3:

            @pl.when(i == 1)
            def _():
                gossip_quarter()
        elif level == 0:

            @pl.when(i < 2)
            def _():
                @pl.loop(5 * i, 5 * i + 5)
                def _(t):
                    gossip_half(t)

            @pl.when(jnp.logical_and(i == 3, c == 1))
            def _():
                @pl.loop(0, NT)
                def _(t):
                    arrived(gbuf.at[t], br.at[t], 140)
                    pass_on(t).start()
        elif level in (1, 2):

            @pl.when(i < 2)
            def _():
                @pl.loop(4 + 3 * i, 7 + 3 * i)
                def _(t):
                    gossip_half(t)

            if level == 2:

                @pl.when(i == 2)
                def _():
                    for k in range(2):
                        arrived(rel.at[k], ar.at[NT + k], 141 + k)
                        next_leg(k).start()
        else:

            @pl.when(i < 5)
            def _():
                @pl.loop(2 * i, 2 * i + 2)
                def _(t):
                    gossip_half(t)

        @pl.when(i == 4)
        def _():
            m_load.wait()
            if level == 3:
                for d in range(1, 4):
                    arrived(hb.at[:, part(lax.rem(member + 4 - d, 4))], br.at[d - 1], 130)

        @pl.when(i >= 4)
        def _():
            @pl.loop(0, 2)
            def _(h):
                finish(h * NJ + i - 4)

    @pl.loop(0, 2)
    def _(k):
        @pl.when(jnp.logical_not(jnp.logical_and(home, c == k)))
        def _():
            x_send(k).wait_send()

        x_on(k).wait_send()

    m_give.wait_send()
    pl.when(away)(m_keep.wait_send)

    @pl.loop(0, NJ)
    def _(j):
        @pl.when(away)
        def _():
            w_keep(j).wait_send()
            t_keep(j).wait_send()
            h_keep(j).wait_send()

        for copy in (w_give(j), t_give(j), h_give(j), w_own_on(own_rows(j), j), w_o_on(j), p_copy(j), r_copy(j),
                     g_copy(j, 0), g_copy(j, 1)):
            copy.wait_send()

    @pl.loop(*first_copies)
    def _(t):
        a_copy(t).wait_send()

    if level == 0:

        @pl.when(c == 1)
        def _():
            @pl.loop(0, NT)
            def _(t):
                b_copy(t).wait_send()
                pass_on(t).wait_send()
    else:

        @pl.loop(*second_copies)
        def _(t):
            b_copy(t).wait_send()

        if level == 2:
            for k in range(2):
                next_leg(k).wait_send()

    @pl.loop(0, NT)
    def _(t):
        out_w(t).wait()
        out_m(t).wait()


def update(level, rate, tokens, goals, marks, shard, momentum):
    dma = pltpu.SemaphoreType.DMA
    anywhere = pl.BlockSpec(memory_space=pl.ANY)
    vm = pltpu.VMEM
    return pl.pallas_call(
        functools.partial(kernel, level),
        out_shape=(
            jax.ShapeDtypeStruct((ROWS, NT * COLS), F32),
            jax.ShapeDtypeStruct((ROWS, NT * COLS), BF),
        ),
        in_specs=[pl.BlockSpec(memory_space=pltpu.SMEM)] + [anywhere] * 5,
        out_specs=(anywhere, anywhere),
        scratch_shapes=[
            vm((NT, ROWS, COLS), F32),
            vm((NT, ROWS, COLS), BF),
            vm((ROWS, NT * COLS), BF),
            vm((4, SEQ, HALF), BF),
            vm((HALF, 4 * SEQ), BF),
            vm((NJ, 2 * SEQ, COLS), BF),
            vm((2 * SEQ, 128), BF),
            vm((NJ, HALF, COLS), BF),
            vm((NJ, 2 * SEQ, COLS), F32),
            vm((NJ, 2 * SEQ, COLS), BF),
            vm((NJ, 2 * SEQ, COLS), BF),
            vm((NJ, 4 * SEQ, COLS), BF),
            vm((NJ, 2 * ROWS, COLS), BF),
            vm((NJ, 2 * ROWS, COLS), F32),
            vm((NJ, 2 * ROWS, COLS), BF),
            vm((NJ, 2 * ROWS, COLS), BF),
            vm((NT, ROWS, COLS), BF),
            vm((NT, ROWS, COLS), BF),
            vm((NT, ROWS, COLS), BF),
            vm((NT, ROWS, COLS), BF),
            vm((2, ROWS, COLS), BF),
            dma((NT + 1,)),
            dma((2,)), dma((2,)),
            dma((2,)), dma((2,)),
            dma((2, NJ)), dma((2, NJ)),
            dma((2,)), dma((2,)),
            dma((2, NJ)), dma((2, NJ)),
            dma((2, NJ)), dma((2, NJ)),
            dma((NJ,)), dma((NJ,)),
            dma((NJ,)), dma((NJ,)),
            dma((2, NJ)), dma((2, NJ)),
            dma((2, NJ)), dma((NT,)),
            dma((2 * NT,)), dma((2 * NT,)),
            dma((NT,)), dma((NT,)),
            dma((2, NT)),
        ],
        compiler_params=pltpu.CompilerParams(
            collective_id=level, has_side_effects=True, vmem_limit_bytes=60 * 2**20
        ),
        name=f"update_{level}",
    )(rate, tokens, goals, marks, shard, momentum)


def local(inputs, targets, masked, step_index, weights, momentum):
    marks = jnp.broadcast_to((masked[0].astype(F32) / 2048.0).astype(BF)[:, None], (SEQ, 128))
    rate = ((step_index.astype(F32) + 1.0) / 500.0).reshape(1)
    branches = [functools.partial(update, level) for level in range(5)]
    new_weights, new_momentum = lax.switch(
        step_index % 5, branches, rate, inputs[0], targets[0], marks, weights[0], momentum[0]
    )
    return new_weights[None], new_momentum[None]


def solution(mesh):
    in_specs = (
        P("replica", "fsdp", None),
        P("replica", "fsdp", None),
        P("replica", "fsdp"),
        P(),
        P("replica", "fsdp", None),
        P("replica", "fsdp", None),
    )
    out_specs = (P("replica", "fsdp", None), P("replica", "fsdp", None))
    return jax.shard_map(local, mesh=mesh, in_specs=in_specs, out_specs=out_specs, check_vma=False)
```
